256 devices in a mesh: pipe: 8 (over x, core), expert: 32 (over z, y).
Axes of the slice: x: 4, y: 4, z: 8, core: 2. Of those that a mesh axis runs over, the one named last changes fastest.
Arguments:
- inputs: bfloat16 [16, 256, 7168], P(None, 'expert'), may hold values from -6 to 6
- norm_gains: float32 [8, 7168], P('pipe'), may hold values from 0.25 to 1.75
- w_gate: bfloat16 [8, 7168, 4096], P('pipe', None, 'expert'), may hold values from -0.0625 to 0.0625
- w_up: bfloat16 [8, 7168, 4096], P('pipe', None, 'expert'), may hold values from -0.0625 to 0.0625
- w_down: bfloat16 [8, 4096, 7168], P('pipe', 'expert'), may hold values from -0.1875 to 0.1875
- expert_ids: int32 [8, 16, 256, 1], P('pipe', None, 'expert'), may hold values from 0 to 3; in each aligned block of 8 rows (0 to 7, 8 to 15, ..., all dimensions but the last counted through in order) at most 2 rows name the same one
- gate_weights: float32 [8, 16, 256], P('pipe', None, 'expert'), may hold values from 0.2 to 1.5
Outputs:
- states: bfloat16 [8, 16, 256, 7168], P('pipe', None, 'expert')
The draws below stay inside these ranges and needn't reach their ends.
Inputs may be any that keep to these rules, and one draw needn't show every extreme that they name: `expert_ids`: of the tokens of one micro-batch on one device (aligned blocks of 8 tokens), exactly 2 are routed to each expert.
All inputs are finite; a program needn't handle non-finite values.
Results may differ from the reference program's by a relative error of at most 0.03.
Values may be sent and summed in bfloat16 or wider, within the bound.
A program may use at most 64 MiB of HBM per device.

```python
import math
import jax
import jax.numpy as jnp
import numpy as np
from jax import lax

D = 7168
EH = 1024
GROUP = 8
ROWS_DEV = 8
MICRO = 16
LAYERS = 8
EXPERTS = 4
EH_DEV = 128
TOKENS = 256
CAP = 2


def block_levels(stream_key, shape, split, smallest, top_value):
    def one(axis_at, parts):
        heights = jax.random.uniform(jax.random.fold_in(jax.random.fold_in(stream_key, 6), axis_at), (parts,), jnp.float32, smallest / len(split), top_value / len(split))
        return jnp.repeat(jnp.exp(heights), shape[axis_at] // parts).reshape((-1,) + (1,) * (len(shape) - axis_at - 1))

    loudness = one(*split[0])
    for cut in split[1:]:
        loudness = loudness * one(*cut)
    return loudness


def shared_out(own_key, own, number, rows, number_of, top, bound, slope):
    order = jax.random.permutation(own_key, number_of)
    crowded, ordinary = load_shares(number_of, rows * top, bound, slope, True), load_shares(number_of, rows * top, bound, slope, False)
    places = jnp.arange(number_of)

    def named(tallies, offset_by):
        used = int((tallies > 0).sum())
        fixed = max(1, used // 4)
        moved = fixed + (places - fixed + offset_by * (used - fixed)) % max(1, number_of - fixed)
        return jnp.zeros((number_of,), jnp.int32).at[order[jnp.where(places < fixed, places, moved)]].set(jnp.asarray(tallies, jnp.int32))

    tallies = jnp.where(number % 4 == 0, named(crowded, number // 4), named(ordinary, number - number // 4 - 1))
    mixed = jax.random.permutation(jax.random.fold_in(own, 3), number_of)
    source_of, sink = mixed[0:number_of // 2 * 2:2], mixed[1:number_of // 2 * 2:2]
    room = jnp.minimum(tallies[source_of] - 1, bound - tallies[sink]) // 2
    room = jnp.where((source_of == order[0]) | (sink == order[0]) | (tallies[sink] == 0), 0, jnp.maximum(room, 0))
    moved = jax.random.randint(jax.random.fold_in(own, 4), (number_of // 2,), 0, 1 << 20) % (room + 1)
    tallies = tallies.at[source_of].add(-moved).at[sink].add(moved)
    members = jnp.searchsorted(jnp.cumsum(tallies), jnp.arange(rows * top), side="right").astype(jnp.int32)
    table = members.reshape(top, rows).T
    table = table[jax.random.permutation(jax.random.fold_in(own, 1), rows)]
    offset_by = jax.random.randint(jax.random.fold_in(own, 2), (rows, 1), 0, top)
    return jnp.take_along_axis(table, (jnp.arange(top)[None, :] + offset_by) % top, axis=1)


def load_shares(number_of, total, reach, lean, full):
    portions = [(1 << 20) // math.isqrt(grade ** lean) + 1 for grade in range(1, number_of + 1)]
    largest = reach if full else min(reach, max(-(-total // number_of), total * portions[0] // sum(portions)))
    least = 1 if total - largest >= number_of - 1 else 0
    given, surplus = [largest] + [least] * (number_of - 1), total - largest - least * (number_of - 1)
    while surplus > 0:
        movable = [i for i in range(1, number_of) if given[i] < largest] or [i for i in range(1, number_of) if given[i] < reach]
        mass, budget = sum([portions[i] for i in movable]), surplus
        for i in movable:
            extra = min(reach - given[i], max(1, budget * portions[i] // mass), surplus)
            given[i] = given[i] + extra
            surplus = surplus - extra
    return np.array(given)


def centred(rng, extent, scale, limit, cuts=(), dtype=jnp.bfloat16):
    result = jax.random.normal(rng, extent, jnp.float32) * scale
    if len(cuts) > 0:
        result = block_levels(rng, extent, cuts, -0.22, 0.18) * result
    return jnp.clip(result, min=-limit, max=limit).astype(dtype)


def setup_inputs(seed: int = 0) -> dict:
    key_of = jax.random.split(jax.random.key(seed), 8)
    inputs = centred(key_of[0], (MICRO, TOKENS, D), 1.0, 6.0, ((1, 32),))
    norm_gains = jnp.clip(1.0 + 0.15 * jax.random.normal(key_of[1], (LAYERS, D), jnp.float32), 0.25, 1.75)
    w_gate = centred(key_of[2], (LAYERS, D, EXPERTS * EH), D ** -0.5, 0.0625, ((0, 8), (2, 32)))
    w_up = centred(key_of[3], (LAYERS, D, EXPERTS * EH), D ** -0.5, 0.0625, ((0, 8), (2, 32)))
    w_down = centred(key_of[4], (LAYERS, EXPERTS * EH, D), EH ** -0.5, 0.1875, ((0, 8), (1, 32)))
    expert_ids_keys = jax.random.split(jax.random.fold_in(key_of[5], 1), LAYERS * MICRO * TOKENS // ROWS_DEV)
    expert_ids_turns = jax.random.permutation(jax.random.fold_in(key_of[5], 3), LAYERS * MICRO * TOKENS // ROWS_DEV)
    expert_ids = jax.vmap(lambda own, number: shared_out(jax.random.fold_in(key_of[5], 2), own, number, ROWS_DEV, EXPERTS, 1, CAP, 0))(expert_ids_keys, expert_ids_turns).reshape((LAYERS, MICRO, TOKENS, 1))
    gate_weights = jnp.clip(jnp.exp(math.log(1.5) - 2.014903 * jax.random.uniform(key_of[6], (LAYERS, MICRO, TOKENS), jnp.float32) ** block_levels(key_of[6], (LAYERS, MICRO, TOKENS), ((0, 8), (2, 32)), -0.2, 0.2)), 0.2, 1.5)
    return dict(inputs=inputs, norm_gains=norm_gains, w_gate=w_gate, w_up=w_up, w_down=w_down, expert_ids=expert_ids, gate_weights=gate_weights)


def reference(inputs, norm_gains, w_gate, w_up, w_down, expert_ids, gate_weights):
    total_rows = MICRO * TOKENS
    current = inputs.reshape(total_rows, D)
    per_expert = total_rows // EXPERTS
    outputs = []
    for layer in range(LAYERS):
        current32 = current.astype(jnp.float32)
        scale = lax.rsqrt(lax.optimization_barrier(jnp.mean(current32 * current32, axis=-1, keepdims=True)) + 1e-06)
        normed = (current32 * scale * norm_gains[layer]).astype(jnp.bfloat16)
        route = expert_ids[layer].reshape(total_rows).astype(jnp.int32)
        order = jnp.argsort(route, stable=True)
        grouped = normed[order].reshape(EXPERTS, per_expert, D)
        results = []
        for expert in range(EXPERTS):
            first = expert * EH
            gate = jnp.dot(grouped[expert], w_gate[layer][:, first:first + EH], preferred_element_type=jnp.float32)
            upper = jnp.dot(grouped[expert], w_up[layer][:, first:first + EH], preferred_element_type=jnp.float32)
            hidden = (jax.nn.silu(gate) * upper).astype(jnp.bfloat16)
            total = jnp.zeros((per_expert, D), jnp.float32)
            for slice_index in range(GROUP):
                low = slice_index * EH_DEV
                part = jnp.dot(hidden[:, low:low + EH_DEV], w_down[layer][first + low:first + low + EH_DEV, :], preferred_element_type=jnp.float32).astype(jnp.bfloat16)
                part = lax.optimization_barrier(part)
                total = total + part.astype(jnp.float32)
            results.append(total)
        sorted_out = jnp.concatenate(results, axis=0)
        expert_out = jnp.zeros((total_rows, D), jnp.float32).at[order].set(sorted_out)
        weights = gate_weights[layer].reshape(total_rows, 1)
        current = (current32 + weights * expert_out).astype(jnp.bfloat16)
        outputs.append(current.reshape(MICRO, TOKENS, D))
    return jnp.stack(outputs)
```

```python
import functools

import jax
import jax.numpy as jnp
from jax import lax
from jax.experimental import pallas as pl
from jax.experimental.pallas import tpu as pltpu
from jax.sharding import PartitionSpec as P

GROUP = 8
MESH = pl.DeviceIdType.MESH
F32 = jnp.float32
BF16 = jnp.bfloat16


def arrived(ref, sem):
    pltpu.make_async_copy(ref, ref, sem).wait()


def kernel(
    n_pipe, width, inp, wg, wu, wd, gains, table, out,
    gate, up, down, xin, ssin, tabs, perm, perm_t, weight,
    dsend, drecv, rsend, rrecv, own, hbuf, ysend, yrecv, xsend, sssend,
    wsend_sem, wrecv_sem, isend_sem, irecv_sem, tsend_sem, trecv_sem,
    dsend_sem, drecv_sem, rsend_sem, rrecv_sem, hsend_sem, hrecv_sem, ysend_sem, yrecv_sem,
    xsend_sem, xrecv_sem, ssend_sem, srecv_sem, osend_sem, orecv_sem, local_sem,
):
    feat = width // GROUP
    pairs = inp.shape[0] // 16
    s = lax.axis_index("pipe")
    e = lax.axis_index("expert")
    k = e // GROUP
    j = e % GROUP
    here = k * GROUP

    def member(steps):
        return here + lax.rem(j + steps + GROUP, GROUP)

    def other(steps):
        return lax.rem(k + steps + 4, 4) * GROUP + j

    def send(src, dst, send_sem, recv_sem, section, place):
        copy = pltpu.make_async_remote_copy(
            src_ref=src, dst_ref=dst, send_sem=send_sem, recv_sem=recv_sem,
            device_id=(section, place), device_id_type=MESH,
        )
        copy.start()

    barrier = pltpu.get_barrier_semaphore()
    for d in range(1, GROUP):
        pl.semaphore_signal(barrier, inc=1, device_id=(s, member(d)), device_id_type=MESH)
    for d in range(1, 4):
        pl.semaphore_signal(barrier, inc=1, device_id=(s, other(d)), device_id_type=MESH)

    @pl.when(s > 0)
    def _():
        for d in range(GROUP):
            pl.semaphore_signal(barrier, inc=1, device_id=(s - 1, member(d)), device_id_type=MESH)

    @pl.when(s < n_pipe - 1)
    def _():
        for d in range(GROUP):
            pl.semaphore_signal(barrier, inc=1, device_id=(s + 1, member(d)), device_id_type=MESH)

    inner = (s > 0) & (s < n_pipe - 1)

    @pl.when(inner)
    def _():
        pl.semaphore_wait(barrier, 3 * GROUP + 2)

    @pl.when(jnp.logical_not(inner))
    def _():
        pl.semaphore_wait(barrier, 2 * GROUP + 2)

    lane = lax.broadcasted_iota(jnp.int32, (8, 128), 1)
    ids = table[0]
    rank = jnp.zeros((8, 128), F32)
    for step in range(1, 8):
        same = (pltpu.roll(ids, step, 1) == ids) & (lane % 8 >= step)
        rank = rank + jnp.where(same, 1.0, 0.0)
    group_index = k.astype(F32)
    relative = ids - group_index + jnp.where(ids < group_index, 4.0, 0.0)
    block = ((lane % 64) // 8).astype(F32)
    mine = lane // 16 == j
    tabs[0, 0] = jnp.where(mine, relative * 16.0 + block * 2.0 + rank, 0.0)
    tabs[0, 1] = jnp.where(mine, table[1], 0.0)
    tabs[0, 2] = jnp.where(mine, table[2], 0.0)
    for d in range(1, GROUP):
        send(tabs.at[0], tabs.at[d], tsend_sem, trecv_sem, s, member(d))

    def cols(d):
        return pl.ds(pl.multiple_of(lax.rem(j + d, GROUP) * feat, 128), feat)

    half = j // 4
    quarter = j % 4

    @pl.when(s == 0)
    def _():
        for d in range(1, GROUP):
            send(
                inp.at[pl.ds(0, 16), cols(d)], xin.at[half, quarter],
                isend_sem.at[0], irecv_sem.at[0], s, member(d),
            )
        pltpu.make_async_copy(inp.at[pl.ds(0, 16), cols(0)], xin.at[half, quarter], irecv_sem.at[0]).start()

    for d in range(1, GROUP):
        rows = cols(d)
        send(wg.at[rows, :], gate.at[d], wsend_sem.at[0], wrecv_sem.at[0], s, member(d))
        send(wu.at[rows, :], up.at[d], wsend_sem.at[1], wrecv_sem.at[1], s, member(d))
    own_gate = pltpu.make_async_copy(wg.at[cols(0), :], gate.at[0], local_sem.at[0])
    own_up = pltpu.make_async_copy(wu.at[cols(0), :], up.at[0], local_sem.at[1])
    own_down = pltpu.make_async_copy(wd.at[:, cols(0)], down.at[0], local_sem.at[2])
    own_gate.start()
    own_up.start()
    own_down.start()
    for d in range(1, GROUP):
        send(wd.at[:, cols(d)], down.at[d], wsend_sem.at[2], wrecv_sem.at[2], s, member(d))

    @pl.when(s == 0)
    def _():
        @pl.loop(1, pairs)
        def _(p):
            rows = pl.ds(pl.multiple_of(p * 16, 16), 16)
            for d in range(1, GROUP):
                send(
                    inp.at[rows, cols(d)], xin.at[2 * p + half, quarter],
                    isend_sem.at[p], irecv_sem.at[p], s, member(d),
                )
            pltpu.make_async_copy(inp.at[rows, cols(0)], xin.at[2 * p + half, quarter], irecv_sem.at[p]).start()

    arrived(tabs.at[pl.ds(1, 7)], trecv_sem)
    total = tabs[0]
    for d in range(1, GROUP):
        total = total + tabs[d]
    sub64 = lax.broadcasted_iota(jnp.int32, (64, 64), 0)
    lane64 = lax.broadcasted_iota(jnp.int32, (64, 64), 1)
    eye = sub64 == lane64
    arrived(tabs.at[pl.ds(1, 7)], tsend_sem)
    tabs[0] = total

    @pl.loop(0, pairs)
    def _(p):
        for h in range(2):
            u = 2 * p + h
            rows = []
            for field in range(3):
                row = tabs[0, field, pl.ds(p, 1), :]
                row = jnp.broadcast_to(row, (8, 128))
                if h:
                    row = pltpu.roll(row, 64, 1)
                rows.append(row)
            place = jnp.broadcast_to(rows[0][0:1, 0:64], (64, 64))
            scale = jnp.broadcast_to(rows[1][0:1, 0:64], (64, 64))
            perm[u] = jnp.where(place == sub64.astype(F32), 1.0, 0.0).astype(BF16)
            place_col = jnp.sum(jnp.where(eye, place, 0.0), axis=1, keepdims=True)
            perm_t[u] = jnp.where(place_col == lane64.astype(F32), 1.0, 0.0).astype(BF16)
            weight[u] = jnp.sum(jnp.where(eye, scale, 0.0), axis=1, keepdims=True)

            @pl.when(s == 0)
            def _():
                ssin[u] = jnp.zeros((GROUP, 8, 128), F32)
                ssin[u, 0] = rows[2]

    def home_out(h, p):
        u = 2 * p + h

        @pl.when(s > 0)
        def _():
            arrived(xin.at[u], xrecv_sem.at[u])
            arrived(ssin.at[u], srecv_sem.at[u])

        squares = ssin[u, 0]
        for d in range(1, GROUP):
            squares = squares + ssin[u, d]
        row = jnp.broadcast_to(squares[0:1, 0:64], (64, 64))
        col = jnp.sum(jnp.where(eye, row, 0.0), axis=1, keepdims=True)
        scale = lax.rsqrt(col * (1.0 / width) + 1e-06)
        normed = (xin[u].reshape(64, feat).astype(F32) * scale * gains[pl.ds(j, 1), :]).astype(BF16)
        ordered = jnp.dot(perm[u], normed, preferred_element_type=F32).astype(BF16)
        dsend[h] = ordered.reshape(4, 16, feat)
        for d in range(1, 4):
            send(dsend.at[h, d], drecv.at[h, d], dsend_sem.at[h], drecv_sem.at[h], s, other(d))
        drecv[h, 0] = dsend[h, 0]

    def first_products(h):
        arrived(drecv.at[h, pl.ds(1, 3)], drecv_sem.at[h])
        tokens = drecv[h].reshape(64, feat)
        for d in (4, 3, 5, 2, 6, 1, 7, 0):
            both = jnp.concatenate([gate[d], up[d]], axis=1)
            part = jnp.dot(tokens, both, preferred_element_type=F32)
            if d:
                rsend[h, d - 1] = part.astype(BF16)
                send(rsend.at[h, d - 1], rrecv.at[h, d - 1], rsend_sem.at[h], rrecv_sem.at[h], s, member(-d))
            else:
                own[h] = part

    def hidden_units(h):
        arrived(rrecv.at[h], rrecv_sem.at[h])
        both = own[h]
        for d in range(7):
            both = both + rrecv[h, d].astype(F32)
        value = both[:, 0:128]
        hidden = (value / (1.0 + jnp.exp(-value)) * both[:, 128:256]).astype(BF16)
        hbuf[h, 0] = hidden
        for d in (4, 3, 5, 2, 6, 1, 7):
            send(hbuf.at[h, 0], hbuf.at[h, d], hsend_sem.at[h], hrecv_sem.at[h], s, member(d))

    def second_product(h):
        arrived(hbuf.at[h, pl.ds(1, 7)], hrecv_sem.at[h])
        hidden = jnp.concatenate([hbuf[h, d] for d in range(GROUP)], axis=1)
        part = jnp.dot(hidden, down[...].reshape(GROUP * 128, feat), preferred_element_type=F32)
        ysend[h] = part.astype(BF16).reshape(4, 16, feat)
        for d in range(1, 4):
            send(ysend.at[h, d], yrecv.at[h, d], ysend_sem.at[h], yrecv_sem.at[h], s, other(-d))
        yrecv[h, 0] = ysend[h, 0]

    def home_in(h, p):
        u = 2 * p + h
        arrived(yrecv.at[h, pl.ds(1, 3)], yrecv_sem.at[h])
        gathered = jnp.dot(perm_t[u], yrecv[h].reshape(64, feat), preferred_element_type=F32)
        fresh = (xin[u].reshape(64, feat).astype(F32) + weight[u] * gathered).astype(BF16)
        xsend[h] = fresh.reshape(4, 16, feat)

        @pl.when(s < n_pipe - 1)
        def _():
            send(xsend.at[h], xin.at[u], xsend_sem.at[h], xrecv_sem.at[u], s + 1, e)
            wide = fresh.astype(F32)
            squares = wide * wide
            acc = squares[:, 0:128]
            for c in range(1, feat // 128):
                acc = acc + squares[:, c * 128:(c + 1) * 128]
            col = jnp.sum(acc, axis=1, keepdims=True)
            row = jnp.sum(jnp.where(eye, jnp.broadcast_to(col, (64, 64)), 0.0), axis=0, keepdims=True)
            row = jnp.concatenate([row, row], axis=1)
            sssend[h] = jnp.broadcast_to(row, (8, 128))
            for d in range(GROUP):
                send(sssend.at[h], ssin.at[u, d], ssend_sem.at[h], srecv_sem.at[u], s + 1, member(d))

        rows = pl.ds(pl.multiple_of(p * 16, 16), 16)
        for q in range(4):
            m = 4 * h + q

            @pl.when(m == j)
            def _():
                pltpu.make_async_copy(xsend.at[h, q], out.at[rows, cols(0)], osend_sem.at[h]).start()

            @pl.when(m != j)
            def _():
                send(xsend.at[h, q], out.at[rows, cols(0)], osend_sem.at[h], orecv_sem.at[p], s, here + m)

    own_gate.wait()
    own_up.wait()
    arrived(gate.at[pl.ds(1, 7)], wrecv_sem.at[0])
    arrived(up.at[pl.ds(1, 7)], wrecv_sem.at[1])
    own_down.wait()
    arrived(down.at[pl.ds(1, 7)], wrecv_sem.at[2])

    @pl.loop(0, pairs)
    def _(p):
        @pl.when(s == 0)
        def _():
            arrived(xin.at[pl.ds(2 * p, 2)], irecv_sem.at[p])

        for h in range(2):
            home_out(h, p)
        for h in range(2):
            first_products(h)
        for h in range(2):
            hidden_units(h)
        for h in range(2):
            second_product(h)
        for h in range(2):
            home_in(h, p)
        for h in range(2):
            arrived(dsend.at[h, pl.ds(1, 3)], dsend_sem.at[h])
            arrived(rsend.at[h], rsend_sem.at[h])
            arrived(hbuf.at[h, pl.ds(1, 7)], hsend_sem.at[h])
            arrived(ysend.at[h, pl.ds(1, 3)], ysend_sem.at[h])
            arrived(xsend.at[h], osend_sem.at[h])

            @pl.when(s < n_pipe - 1)
            def _():
                arrived(xsend.at[h], xsend_sem.at[h])
                arrived(ssin.at[0], ssend_sem.at[h])

    @pl.loop(0, pairs)
    def _(p):
        arrived(out.at[pl.ds(pl.multiple_of(p * 16, 16), 16), pl.ds(0, 7 * feat)], orecv_sem.at[p])

        @pl.when(s == 0)
        def _():
            arrived(inp.at[pl.ds(pl.multiple_of(p * 16, 16), 16), pl.ds(0, 7 * feat)], isend_sem.at[p])

    arrived(gate.at[pl.ds(1, 7)], wsend_sem.at[0])
    arrived(up.at[pl.ds(1, 7)], wsend_sem.at[1])
    arrived(down.at[pl.ds(1, 7)], wsend_sem.at[2])


def local(inputs, norm_gains, w_gate, w_up, w_down, expert_ids, gate_weights):
    micro, rows, width = inputs.shape
    feat = width // GROUP
    pairs = micro // 2
    units = 2 * pairs
    n_pipe = lax.axis_size("pipe")
    squares = jnp.sum(jnp.square(inputs.astype(F32)), axis=-1)
    fields = jnp.stack([expert_ids[0, :, :, 0].astype(F32), gate_weights[0], squares])
    table = jnp.tile(fields.reshape(3, pairs, 16), (1, 1, 8))
    table = jnp.pad(table, ((0, 0), (0, 8 - pairs), (0, 0)))
    anywhere = pl.BlockSpec(memory_space=pl.ANY)
    vmem = pl.BlockSpec(memory_space=pltpu.VMEM)
    dma = pltpu.SemaphoreType.DMA
    states = pl.pallas_call(
        functools.partial(kernel, n_pipe, width),
        out_shape=jax.ShapeDtypeStruct((micro * rows, width), BF16),
        in_specs=[anywhere] * 4 + [vmem] * 2,
        out_specs=anywhere,
        scratch_shapes=[
            pltpu.VMEM((GROUP, feat, 128), BF16),
            pltpu.VMEM((GROUP, feat, 128), BF16),
            pltpu.VMEM((GROUP, 128, feat), BF16),
            pltpu.VMEM((units, 4, 16, feat), BF16),
            pltpu.VMEM((units, GROUP, 8, 128), F32),
            pltpu.VMEM((GROUP, 3, 8, 128), F32),
            pltpu.VMEM((units, 64, 64), BF16),
            pltpu.VMEM((units, 64, 64), BF16),
            pltpu.VMEM((units, 64, 1), F32),
            pltpu.VMEM((2, 4, 16, feat), BF16),
            pltpu.VMEM((2, 4, 16, feat), BF16),
            pltpu.VMEM((2, 7, 64, 256), BF16),
            pltpu.VMEM((2, 7, 64, 256), BF16),
            pltpu.VMEM((2, 64, 256), F32),
            pltpu.VMEM((2, GROUP, 64, 128), BF16),
            pltpu.VMEM((2, 4, 16, feat), BF16),
            pltpu.VMEM((2, 4, 16, feat), BF16),
            pltpu.VMEM((2, 4, 16, feat), BF16),
            pltpu.VMEM((2, 8, 128), F32),
            dma((3,)), dma((3,)), dma((pairs,)), dma((pairs,)), dma, dma,
            dma((2,)), dma((2,)), dma((2,)), dma((2,)), dma((2,)), dma((2,)), dma((2,)), dma((2,)),
            dma((2,)), dma((units,)), dma((2,)), dma((units,)), dma((2,)), dma((pairs,)), dma((3,)),
        ],
        compiler_params=pltpu.CompilerParams(
            collective_id=0, has_side_effects=True, vmem_limit_bytes=56 * 1024 * 1024
        ),
    )(
        inputs.reshape(micro * rows, width), w_gate[0], w_up[0], w_down[0],
        norm_gains.reshape(GROUP, feat), table,
    )
    return states.reshape(1, micro, rows, width)


def solution(mesh):
    return jax.shard_map(
        local,
        mesh=mesh,
        in_specs=(
            P(None, "expert", None),
            P("pipe", None),
            P("pipe", None, "expert"),
            P("pipe", None, "expert"),
            P("pipe", "expert", None),
            P("pipe", None, "expert", None),
            P("pipe", None, "expert"),
        ),
        out_specs=P("pipe", None, "expert", None),
        check_vma=False,
    )
```

```python
import functools

import jax
import jax.numpy as jnp
from jax import lax
from jax.experimental import pallas as pl
from jax.experimental.pallas import tpu as pltpu
from jax.sharding import PartitionSpec as P

GROUP = 8
MESH = pl.DeviceIdType.MESH
F32 = jnp.float32
BF16 = jnp.bfloat16


def arrived(ref, sem):
    pltpu.make_async_copy(ref, ref, sem).wait()


def kernel(
    n_pipe, width, inp, wg, wu, wd, gains, table, out,
    gate, up, down, xin, xcur, tabs, alltab, allgain, perm, perm_t, weight, obuf,
    sssend, ssin, dsend, drecv, rsend, rrecv, own, psend, precv, hbuf, ysend, yrecv, xsend,
    wsend_sem, wrecv_sem, fsend_sem, frecv_sem, msend_sem, mrecv_sem, isend_sem, irecv_sem,
    tsend_sem, trecv_sem, asend_sem, arecv_sem, gsend_sem, grecv_sem,
    ssend_sem, srecv_sem, dsend_sem, drecv_sem, rsend_sem, rrecv_sem, psend_sem, precv_sem,
    hsend_sem, hrecv_sem, ysend_sem, yrecv_sem, xsend_sem, xrecv_sem, osend_sem, orecv_sem,
    local_sem, go_sem,
):
    feat = width // GROUP
    chips = n_pipe // 2
    s = lax.axis_index("pipe")
    e = lax.axis_index("expert")
    k = e // GROUP
    j = e % GROUP
    here = k * GROUP
    y = j % 4
    parity = j // 4
    chip = s // 2
    core = s % 2
    mate = chip * 2 + 1 - core
    ahead = lax.rem(chip + 1, chips) * 2 + core
    behind = lax.rem(chip + chips - 1, chips) * 2 + core

    def number(steps):
        return lax.rem(parity + steps // 4, 2) * 4 + lax.rem(y + steps, 4)

    def member(steps):
        return here + number(steps)

    def row_member(steps):
        return here + parity * 4 + lax.rem(y + steps + 4, 4)

    def other(steps):
        return lax.rem(k + steps + 4, 4) * GROUP + j

    def cols(d):
        return pl.ds(pl.multiple_of(number(d) * feat, 128), feat)

    def send(src, dst, send_sem, recv_sem, section, place):
        copy = pltpu.make_async_remote_copy(
            src_ref=src, dst_ref=dst, send_sem=send_sem, recv_sem=recv_sem,
            device_id=(section, place), device_id_type=MESH,
        )
        copy.start()

    barrier = pltpu.get_barrier_semaphore()
    for d in range(1, GROUP):
        pl.semaphore_signal(barrier, inc=1, device_id=(s, member(d)), device_id_type=MESH)
    for d in range(1, 4):
        pl.semaphore_signal(barrier, inc=1, device_id=(s, other(d)), device_id_type=MESH)
    for d in range(1, n_pipe):
        pl.semaphore_signal(barrier, inc=1, device_id=(lax.rem(s + d, n_pipe), e), device_id_type=MESH)
    pl.semaphore_wait(barrier, GROUP - 1 + 3 + n_pipe - 1)

    def send_first_weights():
        for d in range(1, GROUP):
            send(wg.at[cols(d), :], gate.at[s, d], wsend_sem.at[0], wrecv_sem.at[0], s, member(d))
            send(wu.at[cols(d), :], up.at[s, d], wsend_sem.at[1], wrecv_sem.at[1], s, member(d))

    def send_last_weights():
        for d in range(1, GROUP):
            send(wd.at[:, cols(d)], down.at[s, d], wsend_sem.at[2], wrecv_sem.at[2], s, member(d))

    pl.when(core == 0)(send_first_weights)
    own_gate = pltpu.make_async_copy(wg.at[cols(0), :], gate.at[s, 0], local_sem.at[0])
    own_up = pltpu.make_async_copy(wu.at[cols(0), :], up.at[s, 0], local_sem.at[1])
    own_down = pltpu.make_async_copy(wd.at[:, cols(0)], down.at[s, 0], local_sem.at[2])
    own_gate.start()
    own_up.start()
    own_down.start()

    my_rows = pl.ds(pl.multiple_of(s * 16, 16), 16)
    half = j // 4
    quarter = j % 4
    for d in range(1, GROUP):
        send(inp.at[my_rows, cols(d)], xin.at[half, quarter], isend_sem, irecv_sem, s, member(d))
    pltpu.make_async_copy(inp.at[my_rows, cols(0)], xin.at[half, quarter], irecv_sem).start()

    lane = lax.broadcasted_iota(jnp.int32, (8, 128), 1)
    ids = table[0]
    rank = jnp.zeros((8, 128), F32)
    for step in range(1, 8):
        same = (pltpu.roll(ids, step, 1) == ids) & (lane % 8 >= step)
        rank = rank + jnp.where(same, 1.0, 0.0)
    group_index = k.astype(F32)
    relative = ids - group_index + jnp.where(ids < group_index, 4.0, 0.0)
    block = ((lane % 64) // 8).astype(F32)
    mine = lane // 16 == j
    tabs[0, 0] = jnp.where(mine, relative * 16.0 + block * 2.0 + rank, 0.0)
    tabs[0, 1] = jnp.where(mine, table[1], 0.0)
    for d in range(1, GROUP):
        send(tabs.at[0], tabs.at[d], tsend_sem, trecv_sem, s, member(d))
    allgain[s] = gains[...]
    for d in range(1, n_pipe):
        send(allgain.at[s], allgain.at[s], gsend_sem, grecv_sem, lax.rem(s + d, n_pipe), e)
    arrived(tabs.at[pl.ds(1, 7)], trecv_sem)
    total = tabs[0]
    for d in range(1, GROUP):
        total = total + tabs[d]
    alltab[s] = total
    for d in range(1, n_pipe):
        send(alltab.at[s], alltab.at[s], asend_sem, arecv_sem, lax.rem(s + d, n_pipe), e)

    sub64 = lax.broadcasted_iota(jnp.int32, (64, 64), 0)
    lane64 = lax.broadcasted_iota(jnp.int32, (64, 64), 1)
    eye = sub64 == lane64
    arrived(alltab.at[pl.ds(0, n_pipe - 1)], arecv_sem)
    arrived(allgain.at[pl.ds(0, n_pipe - 1)], grecv_sem)

    @pl.loop(0, n_pipe)
    def _(m):
        for h in range(2):
            rows = []
            for field in range(2):
                row = jnp.broadcast_to(alltab[m, field, pl.ds(s, 1), :], (8, 128))
                if h:
                    row = pltpu.roll(row, 64, 1)
                rows.append(jnp.broadcast_to(row[0:1, 0:64], (64, 64)))
            place, scale = rows
            perm[m, h] = jnp.where(place == sub64.astype(F32), 1.0, 0.0).astype(BF16)
            place_col = jnp.sum(jnp.where(eye, place, 0.0), axis=1, keepdims=True)
            perm_t[m, h] = jnp.where(place_col == lane64.astype(F32), 1.0, 0.0).astype(BF16)
            weight[m, h] = jnp.sum(jnp.where(eye, scale, 0.0), axis=1, keepdims=True)

    def slot(m, h):
        return lax.rem(m, 2) * 2 + h

    def send_squares(h, m, wide):
        b = slot(m, h)
        squares = wide * wide
        acc = squares[:, 0:128]
        for c in range(1, feat // 128):
            acc = acc + squares[:, c * 128:(c + 1) * 128]
        col = jnp.sum(acc, axis=1, keepdims=True)
        row = jnp.sum(jnp.where(eye, jnp.broadcast_to(col, (64, 64)), 0.0), axis=0, keepdims=True)
        row = jnp.broadcast_to(jnp.concatenate([row, row], axis=1), (8, 128))
        sssend[b] = row
        ssin[b, 0] = row
        for d in (6, 2, 5, 7, 1, 3, 4):
            send(sssend.at[b], ssin.at[b, d], ssend_sem.at[b], srecv_sem.at[b], s, member(d))

    arrived(xin, irecv_sem)
    for h in range(2):
        wide = xin[h].reshape(64, feat).astype(F32)
        xcur[h] = wide
        send_squares(h, 0, wide)

    def pass_on(tick):
        @pl.loop(0, chips)
        def _(i):
            m = 2 * i + core
            for way in range(2):
                if way == 0:
                    hops = lax.rem(chip - i + chips, chips)
                    target = ahead
                else:
                    hops = lax.rem(i - chip + chips, chips)
                    target = behind
                cc = tick - 6 * i - hops

                if way == 0:
                    @pl.when((m == s) & (cc == 0))
                    def _():
                        own_gate.wait()
                        own_up.wait()

                        @pl.when(core == 1)
                        def _():
                            arrived(gate.at[s, pl.ds(1, 7)], wrecv_sem.at[0])
                            arrived(up.at[s, pl.ds(1, 7)], wrecv_sem.at[1])

                    @pl.when((m == s) & (cc == 4))
                    def _():
                        own_down.wait()
                        arrived(down.at[s, pl.ds(1, 7)], wrecv_sem.at[2])

                def move(ref, kind):
                    sem = frecv_sem.at[m, 2 * cc + way]

                    @pl.when(hops > 0)
                    def _():
                        arrived(ref, sem)

                    @pl.when(hops < chips - 1)
                    def _():
                        send(ref, ref, fsend_sem.at[i, way, kind // 2], sem, target, e)

                    send(ref, ref, msend_sem.at[i, kind], mrecv_sem.at[m, kind], mate, e)

                @pl.when((cc >= 0) & (cc < 4))
                def _():
                    move((gate, up)[way].at[m, pl.ds(2 * cc, 2)], way)

                @pl.when((cc >= 4) & (cc < 6))
                def _():
                    move(down.at[m, pl.ds(2 * cc - 8 + 4 * way, 2)], 2)

    @pl.when(core == 0)
    def _():
        arrived(gate.at[s, pl.ds(1, 7)], wrecv_sem.at[0])
        arrived(up.at[s, pl.ds(1, 7)], wrecv_sem.at[1])
        send_last_weights()
        pl.semaphore_signal(go_sem, inc=1, device_id=(mate, e), device_id_type=MESH)

        @pl.loop(0, 9)
        def _(tick):
            pass_on(tick)

    @pl.when(core == 1)
    def _():
        pl.semaphore_wait(go_sem, 1)
        send_first_weights()
        send_last_weights()

    def pass_on_beside(m, step):
        @pl.when((core == 0) | (m > 0))
        def _():
            pass_on(9 + 3 * (m - core) + step)

        @pl.when((core == 1) & (m == 0))
        def _():
            @pl.loop(3 * step, 3 * step + 3)
            def _(tick):
                pass_on(tick)

    def home_out(h, m):
        b = slot(m, h)
        arrived(ssin.at[b, pl.ds(1, 7)], srecv_sem.at[b])
        squares = ssin[b, 0]
        for d in range(1, GROUP):
            squares = squares + ssin[b, d]
        row = jnp.broadcast_to(squares[0:1, 0:64], (64, 64))
        col = jnp.sum(jnp.where(eye, row, 0.0), axis=1, keepdims=True)
        scale = lax.rsqrt(col * (1.0 / width) + 1e-06)
        normed = (xcur[h] * scale * allgain[m, pl.ds(j, 1), :]).astype(BF16)
        ordered = jnp.dot(perm[m, h], normed, preferred_element_type=F32).astype(BF16)
        dsend[b] = ordered.reshape(4, 16, feat)
        for d in (2, 1, 3):
            send(dsend.at[b, d], drecv.at[b, d], dsend_sem.at[b], drecv_sem.at[b], s, other(d))
        drecv[b, 0] = dsend[b, 0]

    def first_products(h, m):
        b = slot(m, h)
        arrived(drecv.at[b, pl.ds(1, 3)], drecv_sem.at[b])
        tokens = drecv[b].reshape(64, feat)
        for d in (2, 1, 3, 0):
            for half_at in range(2):
                both = jnp.concatenate([gate[m, 4 * half_at + d], up[m, 4 * half_at + d]], axis=1)
                part = jnp.dot(tokens, both, preferred_element_type=F32)
                if d:
                    rsend[b, d - 1, half_at] = part.astype(BF16)
                else:
                    own[b, half_at] = part
            if d:
                send(rsend.at[b, d - 1], rrecv.at[b, d - 1], rsend_sem.at[b], rrecv_sem.at[b], s, row_member(-d))

    def row_sums(h, m):
        b = slot(m, h)
        arrived(rrecv.at[b], rrecv_sem.at[b])
        for half_at in range(2):
            both = own[b, half_at]
            for d in range(3):
                both = both + rrecv[b, d, half_at].astype(F32)
            own[b, half_at] = both
            psend[b, 1 - half_at] = both.astype(BF16)
        send(psend.at[b], precv.at[b], psend_sem.at[b], precv_sem.at[b], s, member(4))

    def hidden_units(h, m):
        b = slot(m, h)
        arrived(precv.at[b], precv_sem.at[b])
        for half_at in range(2):
            both = own[b, half_at] + precv[b, half_at].astype(F32)
            value = both[:, 0:128]
            hbuf[b, 0, half_at] = (value / (1.0 + jnp.exp(-value)) * both[:, 128:256]).astype(BF16)
        for d in (2, 1, 3):
            send(hbuf.at[b, 0], hbuf.at[b, d], hsend_sem.at[b], hrecv_sem.at[b], s, row_member(d))

    def second_product(h, m):
        b = slot(m, h)
        arrived(hbuf.at[b, pl.ds(1, 3)], hrecv_sem.at[b])
        hidden = jnp.concatenate([hbuf[b, d, half_at] for half_at in range(2) for d in range(4)], axis=1)
        part = jnp.dot(hidden, down[m].reshape(GROUP * 128, feat), preferred_element_type=F32)
        ysend[b] = part.astype(BF16).reshape(4, 16, feat)
        for d in (2, 1, 3):
            send(ysend.at[b, d], yrecv.at[b, d], ysend_sem.at[b], yrecv_sem.at[b], s, other(-d))
        yrecv[b, 0] = ysend[b, 0]

    def home_in(h, m):
        b = slot(m, h)
        arrived(yrecv.at[b, pl.ds(1, 3)], yrecv_sem.at[b])
        gathered = jnp.dot(perm_t[m, h], yrecv[b].reshape(64, feat), preferred_element_type=F32)
        fresh = (xcur[h] + weight[m, h] * gathered).astype(BF16)
        wide = fresh.astype(F32)
        xcur[h] = wide

        @pl.when(m < n_pipe - 1)
        def _():
            send_squares(h, m + 1, wide)

        xsend[b] = fresh.reshape(4, 16, feat)
        for q in range(4):
            owner = 4 * h + q

            @pl.when(owner == j)
            def _():
                pltpu.make_async_copy(xsend.at[b, q], obuf.at[m, :, cols(0)], xsend_sem.at[b]).start()

            @pl.when(owner != j)
            def _():
                send(xsend.at[b, q], obuf.at[m, :, cols(0)], xsend_sem.at[b], xrecv_sem.at[m], s, here + owner)

    def hand_over(m):
        for h in range(2):
            b = slot(m, h)
            arrived(dsend.at[b, pl.ds(1, 3)], dsend_sem.at[b])
            arrived(rsend.at[b], rsend_sem.at[b])
            arrived(psend.at[b], psend_sem.at[b])
            arrived(hbuf.at[b, pl.ds(1, 3)], hsend_sem.at[b])
            arrived(ysend.at[b, pl.ds(1, 3)], ysend_sem.at[b])
            arrived(ssin.at[b, pl.ds(1, 7)], ssend_sem.at[b])
            arrived(xsend.at[b], xsend_sem.at[b])
        arrived(obuf.at[m, :, pl.ds(0, 7 * feat)], xrecv_sem.at[m])

        @pl.when(m == s)
        def _():
            pltpu.make_async_copy(obuf.at[m], out.at[my_rows, :], local_sem.at[3]).start()

        @pl.when(m != s)
        def _():
            send(obuf.at[m], out.at[my_rows, :], osend_sem.at[m], orecv_sem.at[s], m, e)

    @pl.loop(0, n_pipe)
    def _(m):
        for h in range(2):
            home_out(h, m)

        pass_on_beside(m, 0)

        @pl.when(lax.rem(m, 2) != core)
        def _():
            arrived(gate.at[m], mrecv_sem.at[m, 0])
            arrived(up.at[m], mrecv_sem.at[m, 1])

        for h in range(2):
            first_products(h, m)

        @pl.when(m > 0)
        def _():
            hand_over(m - 1)

        for h in range(2):
            row_sums(h, m)

        pass_on_beside(m, 1)

        for h in range(2):
            hidden_units(h, m)

        @pl.when(lax.rem(m, 2) != core)
        def _():
            arrived(down.at[m], mrecv_sem.at[m, 2])

        for h in range(2):
            second_product(h, m)

        pass_on_beside(m, 2)

        for h in range(2):
            home_in(h, m)

    hand_over(n_pipe - 1)

    arrived(tabs.at[pl.ds(1, 7)], tsend_sem)
    arrived(alltab.at[pl.ds(0, n_pipe - 1)], asend_sem)
    arrived(allgain.at[pl.ds(0, n_pipe - 1)], gsend_sem)
    arrived(inp.at[pl.ds(0, 16), pl.ds(0, 7 * feat)], isend_sem)
    arrived(gate.at[s, pl.ds(1, 7)], wsend_sem.at[0])
    arrived(up.at[s, pl.ds(1, 7)], wsend_sem.at[1])
    arrived(down.at[s, pl.ds(1, 7)], wsend_sem.at[2])

    @pl.loop(0, chips)
    def _(i):
        @pl.when(lax.rem(chip - i + chips, chips) < chips - 1)
        def _():
            arrived(gate.at[0], fsend_sem.at[i, 0, 0])
            arrived(down.at[0, pl.ds(0, 4)], fsend_sem.at[i, 0, 1])

        @pl.when(lax.rem(i - chip + chips, chips) < chips - 1)
        def _():
            arrived(up.at[0], fsend_sem.at[i, 1, 0])
            arrived(down.at[0, pl.ds(0, 4)], fsend_sem.at[i, 1, 1])

        arrived(gate.at[0], msend_sem.at[i, 0])
        arrived(up.at[0], msend_sem.at[i, 1])
        arrived(down.at[0], msend_sem.at[i, 2])

    @pl.loop(0, n_pipe)
    def _(m):
        rows = pl.ds(pl.multiple_of(m * 16, 16), 16)

        @pl.when(m == s)
        def _():
            pltpu.make_async_copy(obuf.at[m], out.at[rows, :], local_sem.at[3]).wait()

        @pl.when(m != s)
        def _():
            arrived(obuf.at[m], osend_sem.at[m])
            arrived(out.at[rows, :], orecv_sem.at[m])


def local(inputs, norm_gains, w_gate, w_up, w_down, expert_ids, gate_weights):
    micro, rows, width = inputs.shape
    feat = width // GROUP
    pairs = micro // 2
    n_pipe = lax.axis_size("pipe")
    fields = jnp.stack([expert_ids[0, :, :, 0].astype(F32), gate_weights[0]])
    table = jnp.tile(fields.reshape(2, pairs, 16), (1, 1, 8))
    table = jnp.pad(table, ((0, 0), (0, 8 - pairs), (0, 0)))
    anywhere = pl.BlockSpec(memory_space=pl.ANY)
    vmem = pl.BlockSpec(memory_space=pltpu.VMEM)
    dma = pltpu.SemaphoreType.DMA
    states = pl.pallas_call(
        functools.partial(kernel, n_pipe, width),
        out_shape=jax.ShapeDtypeStruct((micro * rows, width), BF16),
        in_specs=[anywhere] * 4 + [vmem] * 2,
        out_specs=anywhere,
        scratch_shapes=[
            pltpu.VMEM((n_pipe, GROUP, feat, 128), BF16),
            pltpu.VMEM((n_pipe, GROUP, feat, 128), BF16),
            pltpu.VMEM((n_pipe, GROUP, 128, feat), BF16),
            pltpu.VMEM((2, 4, 16, feat), BF16),
            pltpu.VMEM((2, 64, feat), F32),
            pltpu.VMEM((GROUP, 2, 8, 128), F32),
            pltpu.VMEM((n_pipe, 2, 8, 128), F32),
            pltpu.VMEM((n_pipe, GROUP, feat), F32),
            pltpu.VMEM((n_pipe, 2, 64, 64), BF16),
            pltpu.VMEM((n_pipe, 2, 64, 64), BF16),
            pltpu.VMEM((n_pipe, 2, 64, 1), F32),
            pltpu.VMEM((n_pipe, 16, width), BF16),
            pltpu.VMEM((4, 8, 128), F32),
            pltpu.VMEM((4, GROUP, 8, 128), F32),
            pltpu.VMEM((4, 4, 16, feat), BF16),
            pltpu.VMEM((4, 4, 16, feat), BF16),
            pltpu.VMEM((4, 3, 2, 64, 256), BF16),
            pltpu.VMEM((4, 3, 2, 64, 256), BF16),
            pltpu.VMEM((4, 2, 64, 256), F32),
            pltpu.VMEM((4, 2, 64, 256), BF16),
            pltpu.VMEM((4, 2, 64, 256), BF16),
            pltpu.VMEM((4, 4, 2, 64, 128), BF16),
            pltpu.VMEM((4, 4, 16, feat), BF16),
            pltpu.VMEM((4, 4, 16, feat), BF16),
            pltpu.VMEM((4, 4, 16, feat), BF16),
            dma((3,)), dma((3,)), dma((n_pipe // 2, 2, 2)), dma((n_pipe, 12)),
            dma((n_pipe // 2, 3)), dma((n_pipe, 3)), dma, dma,
            dma, dma, dma, dma, dma, dma,
            dma((4,)), dma((4,)), dma((4,)), dma((4,)), dma((4,)), dma((4,)), dma((4,)), dma((4,)),
            dma((4,)), dma((4,)), dma((4,)), dma((4,)), dma((4,)), dma((n_pipe,)), dma((n_pipe,)), dma((n_pipe,)),
            dma((4,)), pltpu.SemaphoreType.REGULAR,
        ],
        compiler_params=pltpu.CompilerParams(
            collective_id=0, has_side_effects=True, vmem_limit_bytes=60 * 1024 * 1024
        ),
    )(
        inputs.reshape(micro * rows, width), w_gate[0], w_up[0], w_down[0],
        norm_gains.reshape(GROUP, feat), table,
    )
    return states.reshape(1, micro, rows, width)


def solution(mesh):
    return jax.shard_map(
        local,
        mesh=mesh,
        in_specs=(
            P(None, "expert", None),
            P("pipe", None),
            P("pipe", None, "expert"),
            P("pipe", None, "expert"),
            P("pipe", "expert", None),
            P("pipe", None, "expert", None),
            P("pipe", None, "expert"),
        ),
        out_specs=P("pipe", None, "expert", None),
        check_vma=False,
    )
```

```python
import functools

import jax
import jax.numpy as jnp
from jax import lax
from jax.experimental import pallas as pl
from jax.experimental.pallas import tpu as pltpu
from jax.sharding import PartitionSpec as P

GROUP = 8
PIECES = 6
SKEW = 2
STRIDE = 4
FIRST = PIECES + 3 * SKEW
MESH = pl.DeviceIdType.MESH
F32 = jnp.float32
BF16 = jnp.bfloat16


def arrived(ref, sem):
    pltpu.make_async_copy(ref, ref, sem).wait()


def kernel(
    n_pipe, width, inp, wg, wu, wd, gains, table, out,
    gate, up, down, xin, xcur, tabs, alltab, allgain, perm, perm_t, weight, obuf,
    sssend, ssin, scsend, screcv, dsend, drecv, rsend, rrecv, own, psend, precv, hbuf, ysend, yrecv, xsend,
    wsend_sem, wrecv_sem, fsend_sem, frecv_sem, msend_sem, mrecv_sem, isend_sem, irecv_sem,
    tsend_sem, trecv_sem, asend_sem, arecv_sem, gsend_sem, grecv_sem,
    ssend_sem, srecv_sem, dsend_sem, drecv_sem, rsend_sem, rrecv_sem, scsend_sem, screcv_sem, psend_sem, precv_sem,
    hsend_sem, hrecv_sem, ysend_sem, yrecv_sem, xsend_sem, xrecv_sem, osend_sem, orecv_sem,
    local_sem, go_sem,
):
    feat = width // GROUP
    chips = n_pipe // 2
    s = lax.axis_index("pipe")
    e = lax.axis_index("expert")
    k = e // GROUP
    j = e % GROUP
    here = k * GROUP
    y = j % 4
    parity = j // 4
    chip = s // 2
    core = s % 2
    mate = chip * 2 + 1 - core
    ahead = lax.rem(chip + 1, chips) * 2 + core
    behind = lax.rem(chip + chips - 1, chips) * 2 + core

    def number(steps):
        return lax.rem(parity + steps // 4, 2) * 4 + lax.rem(y + steps, 4)

    def member(steps):
        return here + number(steps)

    def row_member(steps):
        return here + parity * 4 + lax.rem(y + steps + 4, 4)

    def other(steps):
        return lax.rem(k + steps + 4, 4) * GROUP + j

    def cols(d):
        return pl.ds(pl.multiple_of(number(d) * feat, 128), feat)

    def send(src, dst, send_sem, recv_sem, section, place):
        copy = pltpu.make_async_remote_copy(
            src_ref=src, dst_ref=dst, send_sem=send_sem, recv_sem=recv_sem,
            device_id=(section, place), device_id_type=MESH,
        )
        copy.start()

    barrier = pltpu.get_barrier_semaphore()
    for d in range(1, GROUP):
        pl.semaphore_signal(barrier, inc=1, device_id=(s, member(d)), device_id_type=MESH)
    for d in range(1, 4):
        pl.semaphore_signal(barrier, inc=1, device_id=(s, other(d)), device_id_type=MESH)
    for d in range(1, n_pipe):
        pl.semaphore_signal(barrier, inc=1, device_id=(lax.rem(s + d, n_pipe), e), device_id_type=MESH)
    pl.semaphore_wait(barrier, GROUP - 1 + 3 + n_pipe - 1)

    def send_first_weights():
        for d in range(1, GROUP):
            send(wg.at[cols(d), :], gate.at[s, d], wsend_sem.at[0], wrecv_sem.at[0, d], s, member(d))
            send(wu.at[cols(d), :], up.at[s, d], wsend_sem.at[1], wrecv_sem.at[1, d], s, member(d))

    def send_last_weights():
        for d in range(1, GROUP):
            send(wd.at[:, cols(d)], down.at[s, d], wsend_sem.at[2], wrecv_sem.at[2, d], s, member(d))

    pl.when(core == 0)(send_first_weights)

    own_gate = pltpu.make_async_copy(wg.at[cols(0), :], gate.at[s, 0], local_sem.at[0])
    own_up = pltpu.make_async_copy(wu.at[cols(0), :], up.at[s, 0], local_sem.at[1])
    own_down = pltpu.make_async_copy(wd.at[:, cols(0)], down.at[s, 0], local_sem.at[2])
    own_gate.start()
    own_up.start()
    own_down.start()

    my_rows = pl.ds(pl.multiple_of(s * 16, 16), 16)
    half = j // 4
    quarter = j % 4
    for d in range(1, GROUP):
        send(inp.at[my_rows, cols(d)], xin.at[half, quarter], isend_sem, irecv_sem, s, member(d))
    pltpu.make_async_copy(inp.at[my_rows, cols(0)], xin.at[half, quarter], irecv_sem).start()

    lane = lax.broadcasted_iota(jnp.int32, (8, 128), 1)
    ids = table[0]
    rank = jnp.zeros((8, 128), F32)
    for step in range(1, 8):
        same = (pltpu.roll(ids, step, 1) == ids) & (lane % 8 >= step)
        rank = rank + jnp.where(same, 1.0, 0.0)
    group_index = k.astype(F32)
    relative = ids - group_index + jnp.where(ids < group_index, 4.0, 0.0)
    block = ((lane % 64) // 8).astype(F32)
    mine = lane // 16 == j
    tabs[0, 0] = jnp.where(mine, relative * 16.0 + block * 2.0 + rank, 0.0)
    tabs[0, 1] = jnp.where(mine, table[1], 0.0)
    for d in range(1, GROUP):
        send(tabs.at[0], tabs.at[d], tsend_sem, trecv_sem, s, member(d))
    allgain[s] = gains[...]
    for d in range(1, n_pipe):
        send(allgain.at[s], allgain.at[s], gsend_sem, grecv_sem, lax.rem(s + d, n_pipe), e)
    arrived(tabs.at[pl.ds(1, 7)], trecv_sem)
    total = tabs[0]
    for d in range(1, GROUP):
        total = total + tabs[d]
    alltab[s] = total
    for d in range(1, n_pipe):
        send(alltab.at[s], alltab.at[s], asend_sem, arecv_sem, lax.rem(s + d, n_pipe), e)

    sub64 = lax.broadcasted_iota(jnp.int32, (64, 64), 0)
    lane64 = lax.broadcasted_iota(jnp.int32, (64, 64), 1)
    eye = sub64 == lane64
    arrived(alltab.at[pl.ds(0, n_pipe - 1)], arecv_sem)
    arrived(allgain.at[pl.ds(0, n_pipe - 1)], grecv_sem)

    @pl.loop(0, n_pipe)
    def _(m):
        for h in range(2):
            rows = []
            for field in range(2):
                row = jnp.broadcast_to(alltab[m, field, pl.ds(s, 1), :], (8, 128))
                if h:
                    row = pltpu.roll(row, 64, 1)
                rows.append(jnp.broadcast_to(row[0:1, 0:64], (64, 64)))
            place, scale = rows
            perm[m, h] = jnp.where(place == sub64.astype(F32), 1.0, 0.0).astype(BF16)
            place_col = jnp.sum(jnp.where(eye, place, 0.0), axis=1, keepdims=True)
            perm_t[m, h] = jnp.where(place_col == lane64.astype(F32), 1.0, 0.0).astype(BF16)
            weight[m, h] = jnp.sum(jnp.where(eye, scale, 0.0), axis=1, keepdims=True)

    def slot(m, h):
        return lax.rem(m, 2) * 2 + h

    def send_squares(h, m, wide):
        b = slot(m, h)
        squares = wide * wide
        acc = squares[:, 0:128]
        for c in range(1, feat // 128):
            acc = acc + squares[:, c * 128:(c + 1) * 128]
        col = jnp.sum(acc, axis=1, keepdims=True)
        row = jnp.sum(jnp.where(eye, jnp.broadcast_to(col, (64, 64)), 0.0), axis=0, keepdims=True)
        row = jnp.broadcast_to(jnp.concatenate([row, row], axis=1), (8, 128))
        sssend[b] = row
        ssin[b, 0] = row
        for d in (6, 2, 5, 7, 1, 3, 4):
            send(sssend.at[b], ssin.at[b, d], ssend_sem.at[b], srecv_sem.at[b], s, member(d))

    def pass_on(tick):
        @pl.loop(0, chips)
        def _(i):
            m = 2 * i + core
            for way in range(2):
                if way == 0:
                    hops = lax.rem(chip - i + chips, chips)
                    target = ahead
                else:
                    hops = lax.rem(i - chip + chips, chips)
                    target = behind
                cc = tick - STRIDE * i - SKEW * hops

                def move(array, kind, at, own_copy, own_at):
                    ref = array.at[m, pl.ds(at, 2)]
                    sem = frecv_sem.at[m, 2 * cc + way]

                    @pl.when(hops > 0)
                    def _():
                        arrived(ref, sem)

                    @pl.when(hops == 0)
                    def _():
                        if own_copy is None:
                            arrived(array.at[m, at], wrecv_sem.at[kind, at])
                        else:
                            @pl.when(cc == own_at)
                            def _():
                                own_copy.wait()

                            @pl.when(cc > own_at)
                            def _():
                                arrived(array.at[m, at], wrecv_sem.at[kind, at])
                        arrived(array.at[m, at + 1], wrecv_sem.at[kind, at + 1])

                    @pl.when(hops < chips - 1)
                    def _():
                        send(ref, ref, fsend_sem.at[i, way, kind // 2], sem, target, e)

                    send(ref, ref, msend_sem.at[i, kind], mrecv_sem.at[m, kind], mate, e)

                @pl.when((cc >= 0) & (cc < 4))
                def _():
                    move((gate, up)[way], way, 2 * cc, (own_gate, own_up)[way], 0)

                @pl.when((cc >= 4) & (cc < PIECES))
                def _():
                    move(down, 2, 2 * cc - 8 + 4 * way, own_down if way == 0 else None, 4)

            @pl.when((core == 0) & (i == 0) & (tick == jnp.where(chip == 0, 3, 7)))
            def _():
                send_last_weights()
                pl.semaphore_signal(go_sem, inc=1, device_id=(mate, e), device_id_type=MESH)

    def pass_on_beside(m, step):
        each = STRIDE // 2
        low, high = (0, each // 3, 2 * each // 3, each)[step:step + 2]
        third = FIRST // 3
        first = jnp.where(m < core, third * step, FIRST + each * (m - core) + low)
        last = jnp.where(m < core, third * (step + 1), FIRST + each * (m - core) + high)

        @pl.loop(first, last)
        def _(tick):
            pass_on(tick)

    def home_out(h, m):
        b = slot(m, h)
        scaled = (xcur[h] * allgain[m, pl.ds(j, 1), :]).astype(BF16)
        ordered = jnp.dot(perm[m, h], scaled, preferred_element_type=F32).astype(BF16)
        dsend[b] = ordered.reshape(4, 16, feat)
        for d in (2, 1, 3):
            send(dsend.at[b, d], drecv.at[b, d], dsend_sem.at[b], drecv_sem.at[b], s, other(d))
        drecv[b, 0] = dsend[b, 0]

    def scales_out(h, m):
        b = slot(m, h)
        arrived(ssin.at[b, pl.ds(1, 7)], srecv_sem.at[b])
        squares = ssin[b, 0]
        for d in range(1, GROUP):
            squares = squares + ssin[b, d]
        row = lax.rsqrt(jnp.broadcast_to(squares[0:1, 0:64], (64, 64)) * (1.0 / width) + 1e-06)
        col = jnp.sum(perm[m, h].astype(F32) * row, axis=1, keepdims=True)
        scsend[b] = jnp.broadcast_to(col, (64, 128)).reshape(4, 16, 128)
        for d in (2, 1, 3):
            send(scsend.at[b, d], screcv.at[b, d], scsend_sem.at[b], screcv_sem.at[b], s, other(d))
        screcv[b, 0] = scsend[b, 0]

    def first_products(h, m):
        b = slot(m, h)
        arrived(drecv.at[b, pl.ds(1, 3)], drecv_sem.at[b])
        tokens = drecv[b].reshape(64, feat)
        for d in (2, 1, 3, 0):
            for half_at in range(2):
                both = jnp.concatenate([gate[m, 4 * half_at + d], up[m, 4 * half_at + d]], axis=1)
                part = jnp.dot(tokens, both, preferred_element_type=F32)
                if d:
                    rsend[b, d - 1, half_at] = part.astype(BF16)
                else:
                    own[b, half_at] = part
            if d:
                send(rsend.at[b, d - 1], rrecv.at[b, d - 1], rsend_sem.at[b], rrecv_sem.at[b], s, row_member(-d))

    def row_sums(h, m):
        b = slot(m, h)
        arrived(rrecv.at[b], rrecv_sem.at[b])
        for half_at in range(2):
            both = own[b, half_at]
            for d in range(3):
                both = both + rrecv[b, d, half_at].astype(F32)
            own[b, half_at] = both
            psend[b, 1 - half_at] = both.astype(BF16)
        send(psend.at[b], precv.at[b], psend_sem.at[b], precv_sem.at[b], s, member(4))

    def hidden_units(h, m):
        b = slot(m, h)
        arrived(screcv.at[b, pl.ds(1, 3)], screcv_sem.at[b])
        arrived(precv.at[b], precv_sem.at[b])
        scale = screcv[b].reshape(64, 128)
        for half_at in range(2):
            both = own[b, half_at] + precv[b, half_at].astype(F32)
            value = both[:, 0:128] * scale
            hbuf[b, 0, half_at] = (value / (1.0 + jnp.exp(-value)) * (both[:, 128:256] * scale)).astype(BF16)
        for d in (2, 1, 3):
            send(hbuf.at[b, 0], hbuf.at[b, d], hsend_sem.at[b], hrecv_sem.at[b], s, row_member(d))

    arrived(xin, irecv_sem)
    for h in range(2):
        wide = xin[h].reshape(64, feat).astype(F32)
        xcur[h] = wide
        home_out(h, 0)
        send_squares(h, 0, wide)

    @pl.when(core == 0)
    def _():
        @pl.loop(0, FIRST)
        def _(tick):
            pass_on(tick)

    @pl.when(core == 1)
    def _():
        pl.semaphore_wait(go_sem, 1)
        send_first_weights()
        send_last_weights()

    def second_product(h, m):
        b = slot(m, h)
        arrived(hbuf.at[b, pl.ds(1, 3)], hrecv_sem.at[b])
        hidden = jnp.concatenate([hbuf[b, d, half_at] for half_at in range(2) for d in range(4)], axis=1)
        part = jnp.dot(hidden, down[m].reshape(GROUP * 128, feat), preferred_element_type=F32)
        ysend[b] = part.astype(BF16).reshape(4, 16, feat)
        for d in (2, 1, 3):
            send(ysend.at[b, d], yrecv.at[b, d], ysend_sem.at[b], yrecv_sem.at[b], s, other(-d))
        yrecv[b, 0] = ysend[b, 0]

    def home_in(h, m):
        b = slot(m, h)
        arrived(yrecv.at[b, pl.ds(1, 3)], yrecv_sem.at[b])
        gathered = jnp.dot(perm_t[m, h], yrecv[b].reshape(64, feat), preferred_element_type=F32)
        fresh = (xcur[h] + weight[m, h] * gathered).astype(BF16)
        wide = fresh.astype(F32)
        xcur[h] = wide

        @pl.when(m < n_pipe - 1)
        def _():
            home_out(h, m + 1)
            send_squares(h, m + 1, wide)

        xsend[b] = fresh.reshape(4, 16, feat)
        for q in range(4):
            owner = 4 * h + q

            @pl.when(owner == j)
            def _():
                pltpu.make_async_copy(xsend.at[b, q], obuf.at[m, :, cols(0)], xsend_sem.at[b]).start()

            @pl.when(owner != j)
            def _():
                send(xsend.at[b, q], obuf.at[m, :, cols(0)], xsend_sem.at[b], xrecv_sem.at[m], s, here + owner)

    def drain(m):
        for h in range(2):
            b = slot(m, h)
            arrived(dsend.at[b, pl.ds(1, 3)], dsend_sem.at[b])
            arrived(rsend.at[b], rsend_sem.at[b])
            arrived(scsend.at[b, pl.ds(1, 3)], scsend_sem.at[b])
            arrived(psend.at[b], psend_sem.at[b])
            arrived(hbuf.at[b, pl.ds(1, 3)], hsend_sem.at[b])
            arrived(ysend.at[b, pl.ds(1, 3)], ysend_sem.at[b])
            arrived(ssin.at[b, pl.ds(1, 7)], ssend_sem.at[b])
            arrived(xsend.at[b], xsend_sem.at[b])

    def hand_over(m):
        arrived(obuf.at[m, :, pl.ds(0, 7 * feat)], xrecv_sem.at[m])

        @pl.when(m == s)
        def _():
            pltpu.make_async_copy(obuf.at[m], out.at[my_rows, :], local_sem.at[3]).start()

        @pl.when(m != s)
        def _():
            send(obuf.at[m], out.at[my_rows, :], osend_sem.at[m], orecv_sem.at[s], m, e)

    @pl.loop(0, n_pipe)
    def _(m):
        pass_on_beside(m, 0)

        @pl.when(lax.rem(m, 2) != core)
        def _():
            arrived(gate.at[m], mrecv_sem.at[m, 0])
            arrived(up.at[m], mrecv_sem.at[m, 1])

        for h in range(2):
            first_products(h, m)
        for h in range(2):
            scales_out(h, m)

        pass_on_beside(m, 1)

        for h in range(2):
            row_sums(h, m)

        @pl.when(m > 0)
        def _():
            drain(m - 1)

        done = 2 * (m - n_pipe // 2)

        @pl.when(done >= 0)
        def _():
            hand_over(done)

        @pl.when((done >= 0) & (done + 1 < m))
        def _():
            hand_over(done + 1)

        for h in range(2):
            hidden_units(h, m)

        @pl.when(lax.rem(m, 2) != core)
        def _():
            arrived(down.at[m], mrecv_sem.at[m, 2])

        for h in range(2):
            second_product(h, m)

        pass_on_beside(m, 2)

        for h in range(2):
            home_in(h, m)

    drain(n_pipe - 1)
    hand_over(n_pipe - 1)

    arrived(tabs.at[pl.ds(1, 7)], tsend_sem)
    arrived(alltab.at[pl.ds(0, n_pipe - 1)], asend_sem)
    arrived(allgain.at[pl.ds(0, n_pipe - 1)], gsend_sem)
    arrived(inp.at[pl.ds(0, 16), pl.ds(0, 7 * feat)], isend_sem)
    arrived(gate.at[s, pl.ds(1, 7)], wsend_sem.at[0])
    arrived(up.at[s, pl.ds(1, 7)], wsend_sem.at[1])
    arrived(down.at[s, pl.ds(1, 7)], wsend_sem.at[2])

    @pl.loop(0, chips)
    def _(i):
        @pl.when(lax.rem(chip - i + chips, chips) < chips - 1)
        def _():
            arrived(gate.at[0], fsend_sem.at[i, 0, 0])
            arrived(down.at[0, pl.ds(0, 4)], fsend_sem.at[i, 0, 1])

        @pl.when(lax.rem(i - chip + chips, chips) < chips - 1)
        def _():
            arrived(up.at[0], fsend_sem.at[i, 1, 0])
            arrived(down.at[0, pl.ds(0, 4)], fsend_sem.at[i, 1, 1])

        arrived(gate.at[0], msend_sem.at[i, 0])
        arrived(up.at[0], msend_sem.at[i, 1])
        arrived(down.at[0], msend_sem.at[i, 2])

    @pl.loop(0, n_pipe)
    def _(m):
        rows = pl.ds(pl.multiple_of(m * 16, 16), 16)

        @pl.when(m == s)
        def _():
            pltpu.make_async_copy(obuf.at[m], out.at[rows, :], local_sem.at[3]).wait()

        @pl.when(m != s)
        def _():
            arrived(obuf.at[m], osend_sem.at[m])
            arrived(out.at[rows, :], orecv_sem.at[m])


def local(inputs, norm_gains, w_gate, w_up, w_down, expert_ids, gate_weights):
    micro, rows, width = inputs.shape
    feat = width // GROUP
    pairs = micro // 2
    n_pipe = lax.axis_size("pipe")
    fields = jnp.stack([expert_ids[0, :, :, 0].astype(F32), gate_weights[0]])
    table = jnp.tile(fields.reshape(2, pairs, 16), (1, 1, 8))
    table = jnp.pad(table, ((0, 0), (0, 8 - pairs), (0, 0)))
    anywhere = pl.BlockSpec(memory_space=pl.ANY)
    vmem = pl.BlockSpec(memory_space=pltpu.VMEM)
    dma = pltpu.SemaphoreType.DMA
    states = pl.pallas_call(
        functools.partial(kernel, n_pipe, width),
        out_shape=jax.ShapeDtypeStruct((micro * rows, width), BF16),
        in_specs=[anywhere] * 4 + [vmem] * 2,
        out_specs=anywhere,
        scratch_shapes=[
            pltpu.VMEM((n_pipe, GROUP, feat, 128), BF16),
            pltpu.VMEM((n_pipe, GROUP, feat, 128), BF16),
            pltpu.VMEM((n_pipe, GROUP, 128, feat), BF16),
            pltpu.VMEM((2, 4, 16, feat), BF16),
            pltpu.VMEM((2, 64, feat), F32),
            pltpu.VMEM((GROUP, 2, 8, 128), F32),
            pltpu.VMEM((n_pipe, 2, 8, 128), F32),
            pltpu.VMEM((n_pipe, GROUP, feat), F32),
            pltpu.VMEM((n_pipe, 2, 64, 64), BF16),
            pltpu.VMEM((n_pipe, 2, 64, 64), BF16),
            pltpu.VMEM((n_pipe, 2, 64, 1), F32),
            pltpu.VMEM((n_pipe, 16, width), BF16),
            pltpu.VMEM((4, 8, 128), F32),
            pltpu.VMEM((4, GROUP, 8, 128), F32),
            pltpu.VMEM((4, 4, 16, 128), F32),
            pltpu.VMEM((4, 4, 16, 128), F32),
            pltpu.VMEM((4, 4, 16, feat), BF16),
            pltpu.VMEM((4, 4, 16, feat), BF16),
            pltpu.VMEM((4, 3, 2, 64, 256), BF16),
            pltpu.VMEM((4, 3, 2, 64, 256), BF16),
            pltpu.VMEM((4, 2, 64, 256), F32),
            pltpu.VMEM((4, 2, 64, 256), BF16),
            pltpu.VMEM((4, 2, 64, 256), BF16),
            pltpu.VMEM((4, 4, 2, 64, 128), BF16),
            pltpu.VMEM((4, 4, 16, feat), BF16),
            pltpu.VMEM((4, 4, 16, feat), BF16),
            pltpu.VMEM((4, 4, 16, feat), BF16),
            dma((3,)), dma((3, GROUP)), dma((n_pipe // 2, 2, 2)), dma((n_pipe, 2 * PIECES)),
            dma((n_pipe // 2, 3)), dma((n_pipe, 3)), dma, dma,
            dma, dma, dma, dma, dma, dma,
            dma((4,)), dma((4,)), dma((4,)), dma((4,)), dma((4,)), dma((4,)), dma((4,)), dma((4,)), dma((4,)), dma((4,)),
            dma((4,)), dma((4,)), dma((4,)), dma((4,)), dma((4,)), dma((n_pipe,)), dma((n_pipe,)), dma((n_pipe,)),
            dma((4,)), pltpu.SemaphoreType.REGULAR,
        ],
        compiler_params=pltpu.CompilerParams(
            collective_id=0, has_side_effects=True, vmem_limit_bytes=60 * 1024 * 1024
        ),
    )(
        inputs.reshape(micro * rows, width), w_gate[0], w_up[0], w_down[0],
        norm_gains.reshape(GROUP, feat), table,
    )
    return states.reshape(1, micro, rows, width)


def solution(mesh):
    return jax.shard_map(
        local,
        mesh=mesh,
        in_specs=(
            P(None, "expert", None),
            P("pipe", None),
            P("pipe", None, "expert"),
            P("pipe", None, "expert"),
            P("pipe", "expert", None),
            P("pipe", None, "expert", None),
            P("pipe", None, "expert"),
        ),
        out_specs=P("pipe", None, "expert", None),
        check_vma=False,
    )
```
